256 devices in a mesh: own: 32 (over y, x, core), grp: 8 (over z).
Axes of the slice: x: 4, y: 4, z: 8, core: 2. Of those that a mesh axis runs over, the one named last changes fastest.
Arguments:
- embeddings: bfloat16 [262144, 768], P(('own', 'grp')), may hold values from -6 to 6
- cluster_ids: int32 [262144], P(('own', 'grp')), may hold values from 0 to 511, never falling along the last dimension, each value on 1 to 2048 neighbouring positions
Outputs:
- nearest: float32 [262144], P(('own', 'grp'))
The draws below stay inside these ranges and needn't reach their ends.
Inputs may be any that keep to these rules, and one draw needn't show every extreme that they name: cluster_ids never falls along the rows; every cluster has 1 to 2048 rows and some cluster has exactly 2048.
All inputs are finite; a program needn't handle non-finite values.
Results may differ from the reference program's by a relative error of at most 0.0014.
Values may be sent and summed in bfloat16 or wider, within the bound.
A program may use at most 64 MiB of HBM per device.

```python
import math
import jax
import jax.numpy as jnp
import numpy as np
from jax import lax

D = 768
ROWS_DEV = 1024
SPAN = 2
ROWS = 262144
CLUSTERS = 512


def levels(own_key, shape, pieces, smallest, largest):
    def one(dim, parts):
        heights = jax.random.uniform(jax.random.fold_in(jax.random.fold_in(own_key, 6), dim), (parts,), jnp.float32, smallest / len(pieces), largest / len(pieces))
        return jnp.repeat(jnp.exp(heights), shape[dim] // parts).reshape((-1,) + (1,) * (len(shape) - dim - 1))

    factor_of = one(*pieces[0])
    for cut in pieces[1:]:
        factor_of = factor_of * one(*cut)
    return factor_of


def profile(number_of, total, bound, slope):
    portions = [(1 << 20) // math.isqrt(standing ** slope) + 1 for standing in range(2, number_of + 1)]
    surplus, counts = total - bound - (number_of - 1), [1] * (number_of - 1)
    while surplus > 0:
        movable = [i for i in range(number_of - 1) if counts[i] < bound]
        whole, budget = sum([portions[i] for i in movable]), surplus
        for i in movable:
            addition = min(bound - counts[i], max(1, budget * portions[i] // whole), surplus)
            counts[i] = counts[i] + addition
            surplus = surplus - addition
    return np.array([bound] + counts)


def uneven_parts(stream_key, number_of, total, most, lean):
    if number_of == 2:
        one = jax.random.randint(stream_key, (), max(1, total - most), min(most, total - 1) + 1)
        return jnp.stack([one, total - one])
    tallies = jnp.asarray(profile(number_of, total, most, lean), jnp.int32)
    couples = (number_of - 1) // 2
    giver, taker = tallies[1:1 + 2 * couples:2], tallies[2:2 + 2 * couples:2]
    room = jnp.minimum(giver - 1, most - taker)
    moved = jax.random.randint(jax.random.fold_in(stream_key, 1), (couples,), 0, 1 << 20) % (room + 1)
    tallies = tallies.at[1:1 + 2 * couples:2].set(giver - moved).at[2:2 + 2 * couples:2].set(taker + moved)
    return tallies[jax.random.permutation(jax.random.fold_in(stream_key, 2), number_of)]


def bell_draw(key, shape, scale, reach, shards=(), held_as=jnp.bfloat16):
    result = jax.random.normal(key, shape, jnp.float32) * scale
    if len(shards) > 0:
        result = levels(key, shape, shards, -0.22, 0.18) * result
    return jnp.clip(result, min=-reach, max=reach).astype(held_as)


def setup_inputs(seed: int = 0) -> dict:
    key_list = jax.random.split(jax.random.key(seed), 3)
    embeddings = bell_draw(key_list[0], (ROWS, D), 1.0, 6.0, ((0, 256),))
    cluster_ids = jnp.searchsorted(jnp.cumsum(uneven_parts(key_list[1], CLUSTERS, ROWS, SPAN * ROWS_DEV, 2)), jnp.arange(ROWS), side="right").astype(jnp.int32)
    return {"embeddings": embeddings, "cluster_ids": cluster_ids}


def unit_rows(block):
    values = block.astype(jnp.float32)
    scale = lax.rsqrt(lax.optimization_barrier(jnp.mean(values * values, axis=1, keepdims=True)) + 1e-06)
    return (values * scale * values.shape[1] ** (-0.5)).astype(jnp.bfloat16)

def reference(embeddings, cluster_ids):
    unit = unit_rows(embeddings)
    margin = SPAN * ROWS_DEV
    padded = jnp.pad(unit, ((margin, margin), (0, 0)))
    padded_ids = jnp.pad(cluster_ids, (margin, margin), constant_values=-1)
    rank = jnp.arange(ROWS_DEV, dtype=jnp.int32)

    def one_block(index):
        start = (index * ROWS_DEV).astype(jnp.int32)
        rows_unit = lax.dynamic_slice_in_dim(unit, start, ROWS_DEV, 0)
        rows_ids = lax.dynamic_slice_in_dim(cluster_ids, start, ROWS_DEV, 0)
        best = jnp.full((ROWS_DEV,), -1.0, jnp.float32)
        for offset in range(-SPAN, SPAN + 1):
            begin = (start + margin + offset * ROWS_DEV).astype(jnp.int32)
            other = lax.dynamic_slice_in_dim(padded, begin, ROWS_DEV, 0)
            other_ids = lax.dynamic_slice_in_dim(padded_ids, begin, ROWS_DEV, 0)

            def tile(other=other, other_ids=other_ids, offset=offset):
                scores = lax.dot_general(rows_unit, other, (((1,), (1,)), ((), ())), preferred_element_type=jnp.float32)
                match = rows_ids[:, None] == other_ids[None, :]
                if offset == 0:
                    match = match & (rank[:, None] != rank[None, :])
                return lax.optimization_barrier(jnp.max(jnp.where(match, scores, -1.0), axis=1))

            def nothing():
                return jnp.full((ROWS_DEV,), -1.0, jnp.float32)
            hit = jnp.any(other_ids == rows_ids[0]) | jnp.any(other_ids == rows_ids[ROWS_DEV - 1])
            best = jnp.maximum(best, lax.cond(hit, tile, nothing))
        return best
    blocks = lax.map(one_block, jnp.arange(ROWS // ROWS_DEV, dtype=jnp.int32))
    return blocks.reshape(ROWS)
```

```python
import functools

import jax
import jax.numpy as jnp
from jax import lax
from jax.experimental import pallas as pl
from jax.experimental.pallas import tpu as pltpu
from jax.sharding import PartitionSpec as P

MESH = pl.DeviceIdType.MESH
LANES = 128
NT = (((1,), (1,)), ((), ()))


def as_columns(ids_ref, col_ref):
    for t in range(ids_ref.shape[0]):
        wide = jnp.broadcast_to(ids_ref[t : t + 1, :].astype(jnp.float32), (LANES, LANES))
        col_ref[t * LANES : (t + 1) * LANES, :] = wide.T.astype(jnp.int32)


def fold(masked):
    rows, lanes = masked.shape
    return jnp.max(masked.reshape(rows // 8, 8, lanes), axis=0)


def tile_into(acc, rows, row_ids, cols, col_ids, first, count, diagonal=None):
    scores = lax.dot_general(
        rows, cols[first * LANES : (first + count) * LANES, :], NT, preferred_element_type=jnp.float32
    )
    for t in range(count):
        part = scores[:, t * LANES : (t + 1) * LANES]
        match = row_ids == col_ids[first + t : first + t + 1, :]
        if diagonal is not None:
            rank = lax.broadcasted_iota(jnp.int32, part.shape, 0) + diagonal
            lane = lax.broadcasted_iota(jnp.int32, part.shape, 1) + (first + t) * LANES
            match = match & (rank != lane)
        where = pl.ds((first + t) * LANES, LANES)
        acc[:, where] = jnp.maximum(acc[:, where], fold(jnp.where(match, part, -1.0)))


def kernel(n, inner, x_hbm, ids, out, x, unit, lo, hi, lo_ids, hi_ids, own_col, lo_col, hi_col,
           best, for_lo, for_hi, send_lo, send_hi, from_lo, from_hi,
           load_sem, row_send, row_recv, id_send, id_recv, back_send, back_recv):
    rows, width = unit.shape
    step = LANES
    steps = rows // step
    me = lax.axis_index("own") * inner + lax.axis_index("grp")

    def at(flat):
        return (flat // inner, lax.rem(flat, inner))

    right = at(lax.rem(me + 1, n))
    left = at(lax.rem(me + n - 1, n))

    order = []
    for k in range(steps // 2):
        order += [k, steps - 1 - k]
    loads = {
        c: pltpu.make_async_copy(x_hbm.at[pl.ds(c * step, step)], x.at[pl.ds(c * step, step)], load_sem.at[c])
        for c in range(steps)
    }
    for c in order:
        loads[c].start()

    barrier = pltpu.get_barrier_semaphore()
    for target in (left, right):
        pl.semaphore_signal(barrier, inc=1, device_id=target, device_id_type=MESH)

    def remote(src, dst, send_sem, recv_sem, target):
        return pltpu.make_async_remote_copy(
            src_ref=src, dst_ref=dst, send_sem=send_sem, recv_sem=recv_sem, device_id=target, device_id_type=MESH
        )

    to_right, to_left = [], []
    for k in range(steps):
        up = pl.ds((steps - 1 - k) * step, step)
        down = pl.ds(k * step, step)
        to_right.append(remote(unit.at[up], lo.at[up], row_send.at[0, k], row_recv.at[0, k], right))
        to_left.append(remote(unit.at[down], hi.at[down], row_send.at[1, k], row_recv.at[1, k], left))
    ids_right = remote(ids, lo_ids, id_send.at[0], id_recv.at[0], right)
    ids_left = remote(ids, hi_ids, id_send.at[1], id_recv.at[1], left)

    def normalise(c):
        loads[c].wait()
        where = pl.ds(c * step, step)
        values = x[where, :].astype(jnp.float32)
        scale = lax.rsqrt(jnp.mean(values * values, axis=1, keepdims=True) + 1e-06)
        unit[where, :] = (values * scale * width ** (-0.5)).astype(jnp.bfloat16)

    for k in range(steps // 2):
        normalise(k)
        normalise(steps - 1 - k)
        if k == 0:
            pl.semaphore_wait(barrier, 2)
            ids_right.start()
            ids_left.start()
        to_right[k].start()
        to_left[k].start()
    for k in range(steps // 2, steps):
        to_right[k].start()
        to_left[k].start()

    for acc in (best, for_lo, for_hi):
        acc[...] = jnp.full(acc.shape, -1.0, jnp.float32)
    as_columns(ids, own_col)

    def own_step(c, carry):
        start = pl.multiple_of(c * step, step)
        where = pl.ds(start, step)
        tile_into(best, unit[where, :], own_col[where, :], unit, ids, 0, steps, diagonal=start)
        return carry

    lax.fori_loop(0, steps, own_step, 0)

    ids_right.wait_recv()
    as_columns(lo_ids, lo_col)
    ids_left.wait_recv()
    as_columns(hi_ids, hi_col)

    for k in range(steps):
        up = pl.ds((steps - 1 - k) * step, step)
        down = pl.ds(k * step, step)
        to_right[k].wait_recv()
        to_left[k].wait_recv()
        near = min(k, steps - 1 - k) + 1
        tile_into(for_hi, lo[up, :], lo_col[up, :], hi, hi_ids, 0, near)
        tile_into(for_lo, hi[down, :], hi_col[down, :], lo, lo_ids, steps - near, near)
        near_lo = pl.ds(rows - near * step, near * step)
        near_hi = pl.ds(0, near * step)
        tile_into(for_hi, lo[near_lo, :], lo_col[near_lo, :], hi, hi_ids, k, 1)
        tile_into(for_lo, hi[near_hi, :], hi_col[near_hi, :], lo, lo_ids, steps - 1 - k, 1)
        if k == steps - 1:
            for t in range(steps):
                lane = pl.ds(t * LANES, LANES)
                send_lo[t : t + 1, :] = jnp.max(for_lo[:, lane], axis=0, keepdims=True)
                send_hi[t : t + 1, :] = jnp.max(for_hi[:, lane], axis=0, keepdims=True)
            back_left = remote(send_lo, from_hi, back_send.at[0], back_recv.at[0], left)
            back_right = remote(send_hi, from_lo, back_send.at[1], back_recv.at[1], right)
            back_left.start()
            back_right.start()
        tile_into(best, lo[up, :], lo_col[up, :], unit, ids, 0, steps)
        tile_into(best, hi[down, :], hi_col[down, :], unit, ids, 0, steps)

    for k in range(steps):
        to_right[k].wait_send()
        to_left[k].wait_send()
    ids_right.wait_send()
    ids_left.wait_send()
    back_left.wait()
    back_right.wait()
    for t in range(steps):
        mine = jnp.max(best[:, t * LANES : (t + 1) * LANES], axis=0, keepdims=True)
        out[t : t + 1, :] = jnp.maximum(mine, jnp.maximum(from_lo[t : t + 1, :], from_hi[t : t + 1, :]))


def solution(mesh):
    inner = mesh.shape["grp"]
    n = inner * mesh.shape["own"]

    def per_device(embeddings, cluster_ids):
        rows, width = embeddings.shape
        tiles = rows // LANES
        ids = cluster_ids.reshape(tiles, LANES)
        block = pltpu.VMEM((rows, width), jnp.bfloat16)
        few_ids = pltpu.VMEM((tiles, LANES), jnp.int32)
        col = pltpu.VMEM((rows, LANES), jnp.int32)
        acc = pltpu.VMEM((8, rows), jnp.float32)
        small = pltpu.VMEM((tiles, LANES), jnp.float32)
        dma = pltpu.SemaphoreType.DMA
        out = pl.pallas_call(
            functools.partial(kernel, n, inner),
            out_shape=jax.ShapeDtypeStruct((tiles, LANES), jnp.float32),
            in_specs=[pl.BlockSpec(memory_space=pltpu.HBM), pl.BlockSpec(memory_space=pltpu.VMEM)],
            out_specs=pl.BlockSpec(memory_space=pltpu.VMEM),
            scratch_shapes=[block] * 4 + [few_ids] * 2 + [col] * 3 + [acc] * 3 + [small] * 4
            + [dma((tiles,)), dma((2, tiles)), dma((2, tiles)), dma((2,)), dma((2,)), dma((2,)), dma((2,))],
            compiler_params=pltpu.CompilerParams(
                collective_id=0, has_side_effects=True, vmem_limit_bytes=48 * 1024 * 1024
            ),
        )(embeddings, ids)
        return out.reshape(rows)

    return jax.shard_map(
        per_device,
        mesh=mesh,
        in_specs=(P(("own", "grp"), None), P(("own", "grp"))),
        out_specs=P(("own", "grp")),
        check_vma=False,
    )
```

```python
import functools

import jax
import jax.numpy as jnp
from jax import lax
from jax.experimental import pallas as pl
from jax.experimental.pallas import tpu as pltpu
from jax.sharding import PartitionSpec as P

MESH = pl.DeviceIdType.MESH
LANES = 128
FIRST = 64
ROW = 8
HOLD = 2
LAST = 64
NT = (((1,), (1,)), ((), ()))


def as_columns(ids_ref, col_ref):
    for t in range(ids_ref.shape[0]):
        wide = jnp.broadcast_to(ids_ref[t : t + 1, :].astype(jnp.float32), (LANES, LANES))
        col_ref[t * LANES : (t + 1) * LANES, :] = wide.T.astype(jnp.int32)


def fold(masked):
    rows, lanes = masked.shape
    return jnp.max(masked.reshape(rows // 8, 8, lanes), axis=0)


def tile_into(acc, rows, row_ids, cols, col_ids, first, count, diagonal=None):
    scores = lax.dot_general(
        rows, cols[first * LANES : (first + count) * LANES, :], NT, preferred_element_type=jnp.float32
    )
    for t in range(count):
        part = scores[:, t * LANES : (t + 1) * LANES]
        match = row_ids == col_ids[first + t : first + t + 1, :]
        if diagonal is not None:
            rank = lax.broadcasted_iota(jnp.int32, part.shape, 0) + diagonal
            lane = lax.broadcasted_iota(jnp.int32, part.shape, 1) + (first + t) * LANES
            match = match & (rank != lane)
        where = pl.ds((first + t) * LANES, LANES)
        acc[:, where] = jnp.maximum(acc[:, where], fold(jnp.where(match, part, -1.0)))


def narrow(acc, small):
    for t in range(small.shape[0]):
        small[t : t + 1, :] = jnp.max(acc[:, t * LANES : (t + 1) * LANES], axis=0, keepdims=True)


def unit_rows(raw):
    values = raw.astype(jnp.float32)
    scale = lax.rsqrt(jnp.mean(values * values, axis=1, keepdims=True) + 1e-06)
    return (values * scale * values.shape[1] ** (-0.5)).astype(jnp.bfloat16)


def chunks_of(rows):
    edges = [0, FIRST] + list(range(LANES, rows - LANES + 1, LANES)) + [rows - LAST, rows]
    return list(zip(edges[:-1], edges[1:]))


def kernel(n, inner, x_hbm, ids_hbm, out, x, unit, lo, hi, ids, lo_ids, hi_ids, own_col, lo_col, hi_col,
           best, for_lo, for_hi, send_lo, send_hi, from_lo, from_hi, mine,
           load_sem, row_send, row_recv, id_load, id_send, id_recv, back_send, back_recv):
    rows, width = unit.shape
    tiles = rows // LANES
    chunks = chunks_of(rows)
    own, grp = lax.axis_index("own"), lax.axis_index("grp")
    me = own * inner + grp
    has_left, has_right = me > 0, me < n - 1
    late_right = (grp == inner - 1) & (lax.rem(own, ROW) == ROW - 2)
    late_left = (grp == 0) & (lax.rem(own, ROW) == 1)

    def at(flat):
        return (flat // inner, lax.rem(flat, inner))

    right = at(lax.rem(me + 1, n))
    left = at(lax.rem(me + n - 1, n))

    barrier = pltpu.get_barrier_semaphore()

    @pl.when(has_left)
    def _():
        pl.semaphore_signal(barrier, inc=1, device_id=left, device_id_type=MESH)

    @pl.when(has_right)
    def _():
        pl.semaphore_signal(barrier, inc=1, device_id=right, device_id_type=MESH)

    order = []
    for k in range(tiles // 2):
        order += [tiles - 1 - k, k]
    load_ids = pltpu.make_async_copy(ids_hbm, ids, id_load)
    load_ids.start()
    loads = {}
    for c in order:
        where = pl.ds(c * LANES, LANES)
        loads[c] = pltpu.make_async_copy(x_hbm.at[where], x.at[where], load_sem.at[c])
        loads[c].start()

    def remote(src, dst, send_sem, recv_sem, target):
        return pltpu.make_async_remote_copy(
            src_ref=src, dst_ref=dst, send_sem=send_sem, recv_sem=recv_sem, device_id=target, device_id_type=MESH
        )

    up = [pl.ds(rows - b, b - a) for a, b in chunks]
    down = [pl.ds(a, b - a) for a, b in chunks]
    to_right, to_left = [], []
    for k in range(len(chunks)):
        source = x_hbm if k == 0 else unit
        to_right.append(remote(source.at[up[k]], lo.at[up[k]], row_send.at[0, k], row_recv.at[0, k], right))
        to_left.append(remote(source.at[down[k]], hi.at[down[k]], row_send.at[1, k], row_recv.at[1, k], left))
    ids_right = remote(ids_hbm, lo_ids, id_send.at[0], id_recv.at[0], right)
    ids_left = remote(ids_hbm, hi_ids, id_send.at[1], id_recv.at[1], left)

    inside = has_left & has_right

    @pl.when(inside)
    def _():
        pl.semaphore_wait(barrier, 2)

    @pl.when(jnp.logical_not(inside))
    def _():
        pl.semaphore_wait(barrier, 1)

    def begin(copies, ids_copy):
        copies[0].start()
        ids_copy.start()

    def go_on(copies):
        for copy in copies[1:]:
            copy.start()

    early_right = has_right & jnp.logical_not(late_right)
    early_left = has_left & jnp.logical_not(late_left)
    pl.when(early_right)(lambda: begin(to_right, ids_right))
    pl.when(early_left)(lambda: begin(to_left, ids_left))

    def normalise(c):
        loads[c].wait()
        where = pl.ds(c * LANES, LANES)
        unit[where, :] = unit_rows(x[where, :])

    for c in order:
        normalise(c)
    pl.when(early_right)(lambda: go_on(to_right))
    pl.when(early_left)(lambda: go_on(to_left))

    for acc in (best, for_lo, for_hi):
        acc[...] = jnp.full(acc.shape, -1.0, jnp.float32)
    load_ids.wait()
    as_columns(ids, own_col)

    def own_step(c, carry):
        start = pl.multiple_of(c * LANES, LANES)
        where = pl.ds(start, LANES)
        tile_into(best, unit[where, :], own_col[where, :], unit, ids, 0, tiles, diagonal=start)
        return carry

    lax.fori_loop(0, HOLD, own_step, 0)

    @pl.when(late_right)
    def _():
        begin(to_right, ids_right)
        go_on(to_right)

    @pl.when(late_left)
    def _():
        begin(to_left, ids_left)
        go_on(to_left)

    lax.fori_loop(HOLD, tiles, own_step, 0)

    def missing(ids_ref, back):
        ids_ref[...] = jnp.full(ids_ref.shape, -1, jnp.int32)
        back[...] = jnp.full(back.shape, -1.0, jnp.float32)

    pl.when(jnp.logical_not(has_left))(lambda: missing(lo_ids, from_lo))
    pl.when(jnp.logical_not(has_right))(lambda: missing(hi_ids, from_hi))

    for k, (a, b) in enumerate(chunks):
        pl.when(has_left)(to_right[k].wait_recv)
        pl.when(has_right)(to_left[k].wait_recv)
        if k == 0:

            pl.when(has_left)(ids_right.wait_recv)
            as_columns(lo_ids, lo_col)
            pl.when(has_right)(ids_left.wait_recv)
            as_columns(hi_ids, hi_col)
            lo[up[0], :] = unit_rows(lo[up[0], :])
            hi[down[0], :] = unit_rows(hi[down[0], :])
        near = min(b // LANES, -(-(rows - a) // LANES))
        full = b // LANES - 1
        reach = min(a, rows - full * LANES) if b % LANES == 0 else 0
        lo_rows, hi_rows = pl.ds(rows - reach, reach), pl.ds(0, reach)
        if near > 0:
            tile_into(for_hi, lo[up[k], :], lo_col[up[k], :], hi, hi_ids, 0, near)
        if reach > 0:
            tile_into(for_hi, lo[lo_rows, :], lo_col[lo_rows, :], hi, hi_ids, full, 1)
        if b == rows:
            narrow(for_hi, send_hi)
            back_right = remote(send_hi, from_lo, back_send.at[1], back_recv.at[1], right)
            pl.when(has_right)(back_right.start)
        if near > 0:
            tile_into(for_lo, hi[down[k], :], hi_col[down[k], :], lo, lo_ids, tiles - near, near)
        if reach > 0:
            tile_into(for_lo, hi[hi_rows, :], hi_col[hi_rows, :], lo, lo_ids, tiles - 1 - full, 1)
        if b == rows:
            narrow(for_lo, send_lo)
            back_left = remote(send_lo, from_hi, back_send.at[0], back_recv.at[0], left)
            pl.when(has_left)(back_left.start)
        tile_into(best, lo[up[k], :], lo_col[up[k], :], unit, ids, 0, tiles)
        tile_into(best, hi[down[k], :], hi_col[down[k], :], unit, ids, 0, tiles)

    narrow(best, mine)

    @pl.when(has_right)
    def _():
        for copy in to_right + [ids_right]:
            copy.wait_send()
        back_right.wait_send()

    @pl.when(has_left)
    def _():
        for copy in to_left + [ids_left]:
            copy.wait_send()
        back_left.wait_send()

    pl.when(has_right)(back_left.wait_recv)
    pl.when(has_left)(back_right.wait_recv)
    out[...] = jnp.maximum(mine[...], jnp.maximum(from_lo[...], from_hi[...]))


def solution(mesh):
    inner = mesh.shape["grp"]
    n = inner * mesh.shape["own"]

    def per_device(embeddings, cluster_ids):
        rows, width = embeddings.shape
        tiles = rows // LANES
        parts = len(chunks_of(rows))
        ids = cluster_ids.reshape(tiles, LANES)
        block = pltpu.VMEM((rows, width), jnp.bfloat16)
        few_ids = pltpu.VMEM((tiles, LANES), jnp.int32)
        col = pltpu.VMEM((rows, LANES), jnp.int32)
        acc = pltpu.VMEM((8, rows), jnp.float32)
        small = pltpu.VMEM((tiles, LANES), jnp.float32)
        dma = pltpu.SemaphoreType.DMA
        out = pl.pallas_call(
            functools.partial(kernel, n, inner),
            out_shape=jax.ShapeDtypeStruct((tiles, LANES), jnp.float32),
            in_specs=[pl.BlockSpec(memory_space=pltpu.HBM)] * 2,
            out_specs=pl.BlockSpec(memory_space=pltpu.VMEM),
            scratch_shapes=[block] * 4 + [few_ids] * 3 + [col] * 3 + [acc] * 3 + [small] * 5
            + [dma((tiles,)), dma((2, parts)), dma((2, parts)), dma, dma((2,)), dma((2,)), dma((2,)), dma((2,))],
            compiler_params=pltpu.CompilerParams(
                collective_id=0, has_side_effects=True, vmem_limit_bytes=63 * 1024 * 1024
            ),
        )(embeddings, ids)
        return out.reshape(rows)

    return jax.shard_map(
        per_device,
        mesh=mesh,
        in_specs=(P(("own", "grp"), None), P(("own", "grp"))),
        out_specs=P(("own", "grp")),
        check_vma=False,
    )
```

```python
import functools

import jax
import jax.numpy as jnp
from jax import lax
from jax.experimental import pallas as pl
from jax.experimental.pallas import tpu as pltpu
from jax.sharding import PartitionSpec as P

MESH = pl.DeviceIdType.MESH
LANES = 128
FIRST = 64
ROW = 8
HOLD = 7
RESUME = 6
LAST = 64
NT = (((1,), (1,)), ((), ()))


def as_columns(ids_ref, col_ref):
    for t in range(ids_ref.shape[0]):
        wide = jnp.broadcast_to(ids_ref[t : t + 1, :].astype(jnp.float32), (LANES, LANES))
        col_ref[t * LANES : (t + 1) * LANES, :] = wide.T.astype(jnp.int32)


def fold(masked):
    rows, lanes = masked.shape
    return jnp.max(masked.reshape(rows // 8, 8, lanes), axis=0)


def tile_into(acc, rows, row_ids, cols, col_ids, first, count, diagonal=None):
    scores = lax.dot_general(
        rows, cols[first * LANES : (first + count) * LANES, :], NT, preferred_element_type=jnp.float32
    )
    for t in range(count):
        part = scores[:, t * LANES : (t + 1) * LANES]
        match = row_ids == col_ids[first + t : first + t + 1, :]
        if diagonal is not None:
            rank = lax.broadcasted_iota(jnp.int32, part.shape, 0) + diagonal
            lane = lax.broadcasted_iota(jnp.int32, part.shape, 1) + (first + t) * LANES
            match = match & (rank != lane)
        where = pl.ds((first + t) * LANES, LANES)
        acc[:, where] = jnp.maximum(acc[:, where], fold(jnp.where(match, part, -1.0)))


def narrow(acc, small):
    for t in range(small.shape[0]):
        small[t : t + 1, :] = jnp.max(acc[:, t * LANES : (t + 1) * LANES], axis=0, keepdims=True)


def unit_rows(raw):
    values = raw.astype(jnp.float32)
    scale = lax.rsqrt(jnp.mean(values * values, axis=1, keepdims=True) + 1e-06)
    return (values * scale * values.shape[1] ** (-0.5)).astype(jnp.bfloat16)


def chunks_of(rows):
    edges = [0, FIRST] + list(range(LANES, rows - LANES + 1, LANES)) + [rows - LAST, rows]
    return list(zip(edges[:-1], edges[1:]))


def kernel(n, inner, x_hbm, ids_hbm, out, x, unit, lo, hi, ids, lo_ids, hi_ids, own_col, lo_col, hi_col,
           best, for_lo, for_hi, send_lo, send_hi, from_lo, from_hi, mine,
           load_sem, row_send, row_recv, id_load, id_send, id_recv, back_send, back_recv):
    rows, width = unit.shape
    tiles = rows // LANES
    chunks = chunks_of(rows)
    own, grp = lax.axis_index("own"), lax.axis_index("grp")
    me = own * inner + grp
    has_left, has_right = me > 0, me < n - 1
    late_left = (grp == 0) & (lax.rem(own, ROW) == 1) & (own > ROW)

    def at(flat):
        return (flat // inner, lax.rem(flat, inner))

    right = at(lax.rem(me + 1, n))
    left = at(lax.rem(me + n - 1, n))

    barrier = pltpu.get_barrier_semaphore()

    @pl.when(has_left)
    def _():
        pl.semaphore_signal(barrier, inc=1, device_id=left, device_id_type=MESH)

    @pl.when(has_right)
    def _():
        pl.semaphore_signal(barrier, inc=1, device_id=right, device_id_type=MESH)

    order = []
    for k in range(tiles // 2):
        order += [tiles - 1 - k, k]
    load_ids = pltpu.make_async_copy(ids_hbm, ids, id_load)
    load_ids.start()
    loads = {}
    for c in order:
        where = pl.ds(c * LANES, LANES)
        loads[c] = pltpu.make_async_copy(x_hbm.at[where], x.at[where], load_sem.at[c])
        loads[c].start()

    def remote(src, dst, send_sem, recv_sem, target):
        return pltpu.make_async_remote_copy(
            src_ref=src, dst_ref=dst, send_sem=send_sem, recv_sem=recv_sem, device_id=target, device_id_type=MESH
        )

    up = [pl.ds(rows - b, b - a) for a, b in chunks]
    down = [pl.ds(a, b - a) for a, b in chunks]
    to_right, to_left = [], []
    for k in range(len(chunks)):
        source = x_hbm if k == 0 else unit
        to_right.append(remote(source.at[up[k]], lo.at[up[k]], row_send.at[0, k], row_recv.at[0, k], right))
        to_left.append(remote(source.at[down[k]], hi.at[down[k]], row_send.at[1, k], row_recv.at[1, k], left))
    ids_right = remote(ids_hbm, lo_ids, id_send.at[0], id_recv.at[0], right)
    ids_left = remote(ids_hbm, hi_ids, id_send.at[1], id_recv.at[1], left)

    inside = has_left & has_right

    @pl.when(inside)
    def _():
        pl.semaphore_wait(barrier, 2)

    @pl.when(jnp.logical_not(inside))
    def _():
        pl.semaphore_wait(barrier, 1)

    def begin(copies, ids_copy):
        copies[0].start()
        ids_copy.start()

    def go_on(copies):
        for copy in copies:
            copy.start()

    pl.when(has_right)(lambda: begin(to_right, ids_right))
    pl.when(has_left)(lambda: begin(to_left, ids_left))

    def normalise(c):
        loads[c].wait()
        where = pl.ds(c * LANES, LANES)
        unit[where, :] = unit_rows(x[where, :])

    for c in order:
        normalise(c)
    pl.when(has_right)(lambda: go_on(to_right[1:]))
    pl.when(has_left)(lambda: go_on(to_left[1:HOLD]))
    pl.when(has_left & jnp.logical_not(late_left))(lambda: go_on(to_left[HOLD:]))

    for acc in (best, for_lo, for_hi):
        acc[...] = jnp.full(acc.shape, -1.0, jnp.float32)
    load_ids.wait()
    as_columns(ids, own_col)

    def own_step(c, carry):
        start = pl.multiple_of(c * LANES, LANES)
        where = pl.ds(start, LANES)
        tile_into(best, unit[where, :], own_col[where, :], unit, ids, 0, tiles, diagonal=start)
        return carry

    lax.fori_loop(0, tiles, own_step, 0)

    def missing(ids_ref, back):
        ids_ref[...] = jnp.full(ids_ref.shape, -1, jnp.int32)
        back[...] = jnp.full(back.shape, -1.0, jnp.float32)

    pl.when(jnp.logical_not(has_left))(lambda: missing(lo_ids, from_lo))
    pl.when(jnp.logical_not(has_right))(lambda: missing(hi_ids, from_hi))

    for k, (a, b) in enumerate(chunks):
        pl.when(has_left)(to_right[k].wait_recv)
        pl.when(has_right)(to_left[k].wait_recv)
        if k == RESUME:
            pl.when(late_left)(lambda: go_on(to_left[HOLD:]))
        if k == 0:

            pl.when(has_left)(ids_right.wait_recv)
            as_columns(lo_ids, lo_col)
            pl.when(has_right)(ids_left.wait_recv)
            as_columns(hi_ids, hi_col)
            lo[up[0], :] = unit_rows(lo[up[0], :])
            hi[down[0], :] = unit_rows(hi[down[0], :])
        near = min(b // LANES, -(-(rows - a) // LANES))
        full = b // LANES - 1
        reach = min(a, rows - full * LANES) if b % LANES == 0 else 0
        lo_rows, hi_rows = pl.ds(rows - reach, reach), pl.ds(0, reach)
        if near > 0:
            tile_into(for_hi, lo[up[k], :], lo_col[up[k], :], hi, hi_ids, 0, near)
        if reach > 0:
            tile_into(for_hi, lo[lo_rows, :], lo_col[lo_rows, :], hi, hi_ids, full, 1)
        if b == rows:
            narrow(for_hi, send_hi)
            back_right = remote(send_hi, from_lo, back_send.at[1], back_recv.at[1], right)
            pl.when(has_right)(back_right.start)
        if near > 0:
            tile_into(for_lo, hi[down[k], :], hi_col[down[k], :], lo, lo_ids, tiles - near, near)
        if reach > 0:
            tile_into(for_lo, hi[hi_rows, :], hi_col[hi_rows, :], lo, lo_ids, tiles - 1 - full, 1)
        if b == rows:
            narrow(for_lo, send_lo)
            back_left = remote(send_lo, from_hi, back_send.at[0], back_recv.at[0], left)
            pl.when(has_left)(back_left.start)
        tile_into(best, lo[up[k], :], lo_col[up[k], :], unit, ids, 0, tiles)
        tile_into(best, hi[down[k], :], hi_col[down[k], :], unit, ids, 0, tiles)

    narrow(best, mine)

    @pl.when(has_right)
    def _():
        for copy in to_right + [ids_right]:
            copy.wait_send()
        back_right.wait_send()

    @pl.when(has_left)
    def _():
        for copy in to_left + [ids_left]:
            copy.wait_send()
        back_left.wait_send()

    pl.when(has_right)(back_left.wait_recv)
    pl.when(has_left)(back_right.wait_recv)
    out[...] = jnp.maximum(mine[...], jnp.maximum(from_lo[...], from_hi[...]))


def solution(mesh):
    inner = mesh.shape["grp"]
    n = inner * mesh.shape["own"]

    def per_device(embeddings, cluster_ids):
        rows, width = embeddings.shape
        tiles = rows // LANES
        parts = len(chunks_of(rows))
        ids = cluster_ids.reshape(tiles, LANES)
        block = pltpu.VMEM((rows, width), jnp.bfloat16)
        few_ids = pltpu.VMEM((tiles, LANES), jnp.int32)
        col = pltpu.VMEM((rows, LANES), jnp.int32)
        acc = pltpu.VMEM((8, rows), jnp.float32)
        small = pltpu.VMEM((tiles, LANES), jnp.float32)
        dma = pltpu.SemaphoreType.DMA
        out = pl.pallas_call(
            functools.partial(kernel, n, inner),
            out_shape=jax.ShapeDtypeStruct((tiles, LANES), jnp.float32),
            in_specs=[pl.BlockSpec(memory_space=pltpu.HBM)] * 2,
            out_specs=pl.BlockSpec(memory_space=pltpu.VMEM),
            scratch_shapes=[block] * 4 + [few_ids] * 3 + [col] * 3 + [acc] * 3 + [small] * 5
            + [dma((tiles,)), dma((2, parts)), dma((2, parts)), dma, dma((2,)), dma((2,)), dma((2,)), dma((2,))],
            compiler_params=pltpu.CompilerParams(
                collective_id=0, has_side_effects=True, vmem_limit_bytes=63 * 1024 * 1024
            ),
        )(embeddings, ids)
        return out.reshape(rows)

    return jax.shard_map(
        per_device,
        mesh=mesh,
        in_specs=(P(("own", "grp"), None), P(("own", "grp"))),
        out_specs=P(("own", "grp")),
        check_vma=False,
    )
```

```python
import functools

import jax
import jax.numpy as jnp
from jax import lax
from jax.experimental import pallas as pl
from jax.experimental.pallas import tpu as pltpu
from jax.sharding import PartitionSpec as P

MESH = pl.DeviceIdType.MESH
LANES = 128
FIRST = 64
ROW = 8
HOLD = 7
RESUME = 6
LAST = 128
NT = (((1,), (1,)), ((), ()))


def as_columns(ids_ref, col_ref):
    for t in range(ids_ref.shape[0]):
        wide = jnp.broadcast_to(ids_ref[t : t + 1, :].astype(jnp.float32), (LANES, LANES))
        col_ref[t * LANES : (t + 1) * LANES, :] = wide.T.astype(jnp.int32)


def fold(masked):
    rows, lanes = masked.shape
    return jnp.max(masked.reshape(rows // 8, 8, lanes), axis=0)


def tile_into(acc, rows, row_ids, cols, col_ids, first, count, diagonal=None):
    scores = lax.dot_general(
        rows, cols[first * LANES : (first + count) * LANES, :], NT, preferred_element_type=jnp.float32
    )
    for t in range(count):
        part = scores[:, t * LANES : (t + 1) * LANES]
        match = row_ids == col_ids[first + t : first + t + 1, :]
        if diagonal is not None:
            rank = lax.broadcasted_iota(jnp.int32, part.shape, 0) + diagonal
            lane = lax.broadcasted_iota(jnp.int32, part.shape, 1) + (first + t) * LANES
            match = match & (rank != lane)
        where = pl.ds((first + t) * LANES, LANES)
        acc[:, where] = jnp.maximum(acc[:, where], fold(jnp.where(match, part, -1.0)))


def narrow(acc, small):
    for t in range(small.shape[0]):
        small[t : t + 1, :] = jnp.max(acc[:, t * LANES : (t + 1) * LANES], axis=0, keepdims=True)


def unit_rows(raw):
    values = raw.astype(jnp.float32)
    scale = lax.rsqrt(jnp.mean(values * values, axis=1, keepdims=True) + 1e-06)
    return (values * scale * values.shape[1] ** (-0.5)).astype(jnp.bfloat16)


def chunks_of(rows):
    edges = [0, FIRST] + list(range(LANES, rows + 1, LANES))
    return list(zip(edges[:-1], edges[1:]))


def kernel(n, inner, x_hbm, ids_hbm, out, x, unit, lo, hi, ids, lo_ids, hi_ids, own_col, lo_col, hi_col,
           best, for_lo, for_hi, send_lo, send_hi, from_lo, from_hi, mine,
           load_sem, row_send, row_recv, id_load, id_send, id_recv, back_send, back_recv):
    rows, width = unit.shape
    tiles = rows // LANES
    chunks = chunks_of(rows)
    own, grp = lax.axis_index("own"), lax.axis_index("grp")
    me = own * inner + grp
    has_left, has_right = me > 0, me < n - 1
    late_left = (grp == 0) & (lax.rem(own, ROW) == 1) & (own > ROW)

    def at(flat):
        return (flat // inner, lax.rem(flat, inner))

    right = at(lax.rem(me + 1, n))
    left = at(lax.rem(me + n - 1, n))

    barrier = pltpu.get_barrier_semaphore()

    @pl.when(has_right)
    def _():
        pl.semaphore_signal(barrier, inc=1, device_id=right, device_id_type=MESH)

    @pl.when(has_left)
    def _():
        pl.semaphore_signal(barrier, inc=1, device_id=left, device_id_type=MESH)

    order = []
    for k in range(tiles // 2):
        order += [tiles - 1 - k, k]
    load_ids = pltpu.make_async_copy(ids_hbm, ids, id_load)
    load_ids.start()
    loads = {}
    for c in order:
        where = pl.ds(c * LANES, LANES)
        loads[c] = pltpu.make_async_copy(x_hbm.at[where], x.at[where], load_sem.at[c])
        loads[c].start()

    def remote(src, dst, send_sem, recv_sem, target):
        return pltpu.make_async_remote_copy(
            src_ref=src, dst_ref=dst, send_sem=send_sem, recv_sem=recv_sem, device_id=target, device_id_type=MESH
        )

    up = [pl.ds(rows - b, b - a) for a, b in chunks]
    down = [pl.ds(a, b - a) for a, b in chunks]
    to_right, to_left = [], []
    for k in range(len(chunks)):
        source = x_hbm if k == 0 else unit
        to_right.append(remote(source.at[up[k]], lo.at[up[k]], row_send.at[0, k], row_recv.at[0, k], right))
        to_left.append(remote(source.at[down[k]], hi.at[down[k]], row_send.at[1, k], row_recv.at[1, k], left))
    ids_right = remote(ids_hbm, lo_ids, id_send.at[0], id_recv.at[0], right)
    ids_left = remote(ids_hbm, hi_ids, id_send.at[1], id_recv.at[1], left)

    inside = has_left & has_right

    @pl.when(inside)
    def _():
        pl.semaphore_wait(barrier, 2)

    @pl.when(jnp.logical_not(inside))
    def _():
        pl.semaphore_wait(barrier, 1)

    def begin(copies, ids_copy):
        ids_copy.start()
        copies[0].start()

    def go_on(copies):
        for copy in copies:
            copy.start()

    pl.when(has_left)(lambda: begin(to_left, ids_left))
    pl.when(has_right)(lambda: begin(to_right, ids_right))

    def normalise(c):
        loads[c].wait()
        where = pl.ds(c * LANES, LANES)
        unit[where, :] = unit_rows(x[where, :])

    for c in order:
        normalise(c)
    pl.when(has_right)(lambda: go_on(to_right[1:]))
    pl.when(has_left)(lambda: go_on(to_left[1:HOLD]))
    pl.when(has_left & jnp.logical_not(late_left))(lambda: go_on(to_left[HOLD:]))

    for acc in (best, for_lo, for_hi):
        acc[...] = jnp.full(acc.shape, -1.0, jnp.float32)
    load_ids.wait()
    as_columns(ids, own_col)

    def own_step(c, carry):
        start = pl.multiple_of(c * LANES, LANES)
        where = pl.ds(start, LANES)
        tile_into(best, unit[where, :], own_col[where, :], unit, ids, 0, tiles, diagonal=start)
        return carry

    lax.fori_loop(0, tiles, own_step, 0)

    def missing(ids_ref, back):
        ids_ref[...] = jnp.full(ids_ref.shape, -1, jnp.int32)
        back[...] = jnp.full(back.shape, -1.0, jnp.float32)

    pl.when(jnp.logical_not(has_left))(lambda: missing(lo_ids, from_lo))
    pl.when(jnp.logical_not(has_right))(lambda: missing(hi_ids, from_hi))

    for k, (a, b) in enumerate(chunks):
        pl.when(has_left)(to_right[k].wait_recv)
        pl.when(has_right)(to_left[k].wait_recv)
        if k == RESUME:
            pl.when(late_left)(lambda: go_on(to_left[HOLD:]))
        if k == 0:

            pl.when(has_left)(ids_right.wait_recv)
            as_columns(lo_ids, lo_col)
            pl.when(has_right)(ids_left.wait_recv)
            as_columns(hi_ids, hi_col)
            lo[up[0], :] = unit_rows(lo[up[0], :])
            hi[down[0], :] = unit_rows(hi[down[0], :])
        near = min(b // LANES, -(-(rows - a) // LANES))
        full = b // LANES - 1
        reach = min(a, rows - full * LANES) if b % LANES == 0 else 0
        lo_rows, hi_rows = pl.ds(rows - reach, reach), pl.ds(0, reach)
        if near > 0:
            tile_into(for_hi, lo[up[k], :], lo_col[up[k], :], hi, hi_ids, 0, near)
        if reach > 0:
            tile_into(for_hi, lo[lo_rows, :], lo_col[lo_rows, :], hi, hi_ids, full, 1)
        if b == rows:
            narrow(for_hi, send_hi)
            back_right = remote(send_hi, from_lo, back_send.at[1], back_recv.at[1], right)
            pl.when(has_right)(back_right.start)
        if near > 0:
            tile_into(for_lo, hi[down[k], :], hi_col[down[k], :], lo, lo_ids, tiles - near, near)
        if reach > 0:
            tile_into(for_lo, hi[hi_rows, :], hi_col[hi_rows, :], lo, lo_ids, tiles - 1 - full, 1)
        if b == rows:
            narrow(for_lo, send_lo)
            back_left = remote(send_lo, from_hi, back_send.at[0], back_recv.at[0], left)
            pl.when(has_left)(back_left.start)
        tile_into(best, lo[up[k], :], lo_col[up[k], :], unit, ids, 0, tiles)
        tile_into(best, hi[down[k], :], hi_col[down[k], :], unit, ids, 0, tiles)

    narrow(best, mine)

    @pl.when(has_right)
    def _():
        for copy in to_right + [ids_right]:
            copy.wait_send()
        back_right.wait_send()

    @pl.when(has_left)
    def _():
        for copy in to_left + [ids_left]:
            copy.wait_send()
        back_left.wait_send()

    pl.when(has_right)(back_left.wait_recv)
    pl.when(has_left)(back_right.wait_recv)
    out[...] = jnp.maximum(mine[...], jnp.maximum(from_lo[...], from_hi[...]))


def solution(mesh):
    inner = mesh.shape["grp"]
    n = inner * mesh.shape["own"]

    def per_device(embeddings, cluster_ids):
        rows, width = embeddings.shape
        tiles = rows // LANES
        parts = len(chunks_of(rows))
        ids = cluster_ids.reshape(tiles, LANES)
        block = pltpu.VMEM((rows, width), jnp.bfloat16)
        few_ids = pltpu.VMEM((tiles, LANES), jnp.int32)
        col = pltpu.VMEM((rows, LANES), jnp.int32)
        acc = pltpu.VMEM((8, rows), jnp.float32)
        small = pltpu.VMEM((tiles, LANES), jnp.float32)
        dma = pltpu.SemaphoreType.DMA
        out = pl.pallas_call(
            functools.partial(kernel, n, inner),
            out_shape=jax.ShapeDtypeStruct((tiles, LANES), jnp.float32),
            in_specs=[pl.BlockSpec(memory_space=pltpu.HBM)] * 2,
            out_specs=pl.BlockSpec(memory_space=pltpu.VMEM),
            scratch_shapes=[block] * 4 + [few_ids] * 3 + [col] * 3 + [acc] * 3 + [small] * 5
            + [dma((tiles,)), dma((2, parts)), dma((2, parts)), dma, dma((2,)), dma((2,)), dma((2,)), dma((2,))],
            compiler_params=pltpu.CompilerParams(
                collective_id=0, has_side_effects=True, vmem_limit_bytes=63 * 1024 * 1024
            ),
        )(embeddings, ids)
        return out.reshape(rows)

    return jax.shard_map(
        per_device,
        mesh=mesh,
        in_specs=(P(("own", "grp"), None), P(("own", "grp"))),
        out_specs=P(("own", "grp")),
        check_vma=False,
    )
```

```python
import functools

import jax
import jax.numpy as jnp
from jax import lax
from jax.experimental import pallas as pl
from jax.experimental.pallas import tpu as pltpu
from jax.sharding import PartitionSpec as P

MESH = pl.DeviceIdType.MESH
LANES = 128
FIRST = 64
ROW = 8
HOLD = 7
RESUME = 6
LAST = 128
NT = (((1,), (1,)), ((), ()))


def as_columns(ids_ref, col_ref):
    for t in range(ids_ref.shape[0]):
        wide = jnp.broadcast_to(ids_ref[t : t + 1, :].astype(jnp.float32), (LANES, LANES))
        col_ref[t * LANES : (t + 1) * LANES, :] = wide.T.astype(jnp.int32)


def fold(masked):
    rows, lanes = masked.shape
    return jnp.max(masked.reshape(rows // 8, 8, lanes), axis=0)


def tile_into(acc, rows, row_ids, cols, col_ids, first, count, diagonal=None):
    scores = lax.dot_general(
        rows, cols[first * LANES : (first + count) * LANES, :], NT, preferred_element_type=jnp.float32
    )
    for t in range(count):
        part = scores[:, t * LANES : (t + 1) * LANES]
        match = row_ids == col_ids[first + t : first + t + 1, :]
        if diagonal is not None:
            rank = lax.broadcasted_iota(jnp.int32, part.shape, 0) + diagonal
            lane = lax.broadcasted_iota(jnp.int32, part.shape, 1) + (first + t) * LANES
            match = match & (rank != lane)
        where = pl.ds((first + t) * LANES, LANES)
        acc[:, where] = jnp.maximum(acc[:, where], fold(jnp.where(match, part, -1.0)))


def narrow(acc, small):
    for t in range(small.shape[0]):
        small[t : t + 1, :] = jnp.max(acc[:, t * LANES : (t + 1) * LANES], axis=0, keepdims=True)


def unit_rows(raw):
    values = raw.astype(jnp.float32)
    scale = lax.rsqrt(jnp.mean(values * values, axis=1, keepdims=True) + 1e-06)
    return (values * scale * values.shape[1] ** (-0.5)).astype(jnp.bfloat16)


def chunks_of(rows):
    edges = [0, FIRST] + list(range(LANES, rows + 1, LANES))
    return list(zip(edges[:-1], edges[1:]))


def kernel(n, inner, x_hbm, ids_hbm, out, x, unit, lo, hi, ids, lo_ids, hi_ids, own_col, lo_col, hi_col,
           best, for_lo, for_hi, send_lo, send_hi, from_lo, from_hi, mine,
           load_sem, row_send, row_recv, id_load, id_send, id_recv, back_send, back_recv):
    rows, width = unit.shape
    tiles = rows // LANES
    chunks = chunks_of(rows)
    own, grp = lax.axis_index("own"), lax.axis_index("grp")
    me = own * inner + grp
    has_left, has_right = me > 0, me < n - 1
    late_left = (grp == 0) & (lax.rem(own, ROW) == 1) & (own > ROW)

    def at(flat):
        return (flat // inner, lax.rem(flat, inner))

    right = at(lax.rem(me + 1, n))
    left = at(lax.rem(me + n - 1, n))

    barrier = pltpu.get_barrier_semaphore()

    @pl.when(has_right)
    def _():
        pl.semaphore_signal(barrier, inc=1, device_id=right, device_id_type=MESH)

    @pl.when(has_left)
    def _():
        pl.semaphore_signal(barrier, inc=1, device_id=left, device_id_type=MESH)

    order = []
    for k in range(tiles // 2):
        order += [tiles - 1 - k, k]
    load_ids = pltpu.make_async_copy(ids_hbm, ids, id_load)
    load_ids.start()
    loads = {}
    for c in order:
        where = pl.ds(c * LANES, LANES)
        loads[c] = pltpu.make_async_copy(x_hbm.at[where], x.at[where], load_sem.at[c])
        loads[c].start()

    def remote(src, dst, send_sem, recv_sem, target):
        return pltpu.make_async_remote_copy(
            src_ref=src, dst_ref=dst, send_sem=send_sem, recv_sem=recv_sem, device_id=target, device_id_type=MESH
        )

    up = [pl.ds(rows - b, b - a) for a, b in chunks]
    down = [pl.ds(a, b - a) for a, b in chunks]
    to_right, to_left = [], []
    for k in range(len(chunks)):
        source = x_hbm if k == 0 else unit
        to_right.append(remote(source.at[up[k]], lo.at[up[k]], row_send.at[0, k], row_recv.at[0, k], right))
        to_left.append(remote(source.at[down[k]], hi.at[down[k]], row_send.at[1, k], row_recv.at[1, k], left))
    ids_right = remote(ids_hbm, lo_ids, id_send.at[0], id_recv.at[0], right)
    ids_left = remote(ids_hbm, hi_ids, id_send.at[1], id_recv.at[1], left)

    inside = has_left & has_right

    @pl.when(inside)
    def _():
        pl.semaphore_wait(barrier, 2)

    @pl.when(jnp.logical_not(inside))
    def _():
        pl.semaphore_wait(barrier, 1)

    def begin(copies, ids_copy):
        ids_copy.start()
        copies[0].start()

    def go_on(copies):
        for copy in copies:
            copy.start()

    pl.when(has_left)(lambda: begin(to_left, ids_left))
    pl.when(has_right)(lambda: begin(to_right, ids_right))

    def normalise(c):
        loads[c].wait()
        where = pl.ds(c * LANES, LANES)
        unit[where, :] = unit_rows(x[where, :])

    for c in order:
        normalise(c)
    pl.when(has_right)(lambda: go_on(to_right[1:]))
    pl.when(has_left)(lambda: go_on(to_left[1:HOLD]))
    pl.when(has_left & jnp.logical_not(late_left))(lambda: go_on(to_left[HOLD:]))

    for acc in (best, for_lo, for_hi):
        acc[...] = jnp.full(acc.shape, -1.0, jnp.float32)
    load_ids.wait()
    as_columns(ids, own_col)

    def own_step(c, carry):
        start = pl.multiple_of(c * LANES, LANES)
        where = pl.ds(start, LANES)
        tile_into(best, unit[where, :], own_col[where, :], unit, ids, 0, tiles, diagonal=start)
        return carry

    lax.fori_loop(0, tiles, own_step, 0)

    def missing(ids_ref, back):
        ids_ref[...] = jnp.full(ids_ref.shape, -1, jnp.int32)
        back[...] = jnp.full(back.shape, -1.0, jnp.float32)

    pl.when(jnp.logical_not(has_left))(lambda: missing(lo_ids, from_lo))
    pl.when(jnp.logical_not(has_right))(lambda: missing(hi_ids, from_hi))

    for k, (a, b) in enumerate(chunks):
        pl.when(has_left)(to_right[k].wait_recv)
        near = min(b // LANES, -(-(rows - a) // LANES))
        if 0 < near * LANES <= a:
            tile_into(for_hi, lo[up[k], :], lo_col[up[k], :], hi, hi_ids, 0, near)
        pl.when(has_right)(to_left[k].wait_recv)
        if k == RESUME:
            pl.when(late_left)(lambda: go_on(to_left[HOLD:]))
        if k == 0:

            pl.when(has_left)(ids_right.wait_recv)
            as_columns(lo_ids, lo_col)
            pl.when(has_right)(ids_left.wait_recv)
            as_columns(hi_ids, hi_col)
            lo[up[0], :] = unit_rows(lo[up[0], :])
            hi[down[0], :] = unit_rows(hi[down[0], :])
        full = b // LANES - 1
        reach = min(a, rows - full * LANES) if b % LANES == 0 else 0
        lo_rows, hi_rows = pl.ds(rows - reach, reach), pl.ds(0, reach)
        if near > 0 and near * LANES > a:
            tile_into(for_hi, lo[up[k], :], lo_col[up[k], :], hi, hi_ids, 0, near)
        if reach > 0:
            tile_into(for_hi, lo[lo_rows, :], lo_col[lo_rows, :], hi, hi_ids, full, 1)
        if b == rows:
            narrow(for_hi, send_hi)
            back_right = remote(send_hi, from_lo, back_send.at[1], back_recv.at[1], right)
            pl.when(has_right)(back_right.start)
        if near > 0:
            tile_into(for_lo, hi[down[k], :], hi_col[down[k], :], lo, lo_ids, tiles - near, near)
        if reach > 0:
            tile_into(for_lo, hi[hi_rows, :], hi_col[hi_rows, :], lo, lo_ids, tiles - 1 - full, 1)
        if b == rows:
            narrow(for_lo, send_lo)
            back_left = remote(send_lo, from_hi, back_send.at[0], back_recv.at[0], left)
            pl.when(has_left)(back_left.start)
        tile_into(best, lo[up[k], :], lo_col[up[k], :], unit, ids, 0, tiles)
        tile_into(best, hi[down[k], :], hi_col[down[k], :], unit, ids, 0, tiles)

    narrow(best, mine)

    @pl.when(has_right)
    def _():
        for copy in to_right + [ids_right]:
            copy.wait_send()
        back_right.wait_send()

    @pl.when(has_left)
    def _():
        for copy in to_left + [ids_left]:
            copy.wait_send()
        back_left.wait_send()

    pl.when(has_right)(back_left.wait_recv)
    pl.when(has_left)(back_right.wait_recv)
    out[...] = jnp.maximum(mine[...], jnp.maximum(from_lo[...], from_hi[...]))


def solution(mesh):
    inner = mesh.shape["grp"]
    n = inner * mesh.shape["own"]

    def per_device(embeddings, cluster_ids):
        rows, width = embeddings.shape
        tiles = rows // LANES
        parts = len(chunks_of(rows))
        ids = cluster_ids.reshape(tiles, LANES)
        block = pltpu.VMEM((rows, width), jnp.bfloat16)
        few_ids = pltpu.VMEM((tiles, LANES), jnp.int32)
        col = pltpu.VMEM((rows, LANES), jnp.int32)
        acc = pltpu.VMEM((8, rows), jnp.float32)
        small = pltpu.VMEM((tiles, LANES), jnp.float32)
        dma = pltpu.SemaphoreType.DMA
        out = pl.pallas_call(
            functools.partial(kernel, n, inner),
            out_shape=jax.ShapeDtypeStruct((tiles, LANES), jnp.float32),
            in_specs=[pl.BlockSpec(memory_space=pltpu.HBM)] * 2,
            out_specs=pl.BlockSpec(memory_space=pltpu.VMEM),
            scratch_shapes=[block] * 4 + [few_ids] * 3 + [col] * 3 + [acc] * 3 + [small] * 5
            + [dma((tiles,)), dma((2, parts)), dma((2, parts)), dma, dma((2,)), dma((2,)), dma((2,)), dma((2,))],
            compiler_params=pltpu.CompilerParams(
                collective_id=0, has_side_effects=True, vmem_limit_bytes=63 * 1024 * 1024
            ),
        )(embeddings, ids)
        return out.reshape(rows)

    return jax.shard_map(
        per_device,
        mesh=mesh,
        in_specs=(P(("own", "grp"), None), P(("own", "grp"))),
        out_specs=P(("own", "grp")),
        check_vma=False,
    )
```
